256 devices in a mesh: mode: 8 (over x, z_lo), pencil: 32 (over y, z_hi, core).
Axes of the slice: x: 4, y: 4, z: 8 (z_hi: 4, z_lo: 2; z = z_hi * 2 + z_lo), core: 2. Of those that a mesh axis runs over, the one named last changes fastest.
Arguments:
- conformation: float32 [16, 6, 512, 4096], P('mode', None, 'pencil'), may hold values from -1 to 3, as said below
- velocity_grad: float32 [8, 512, 4096], P(None, 'pencil'), may hold values from -1 to 1
- counts: int32 [16], replicated, may hold values from 1 to 12, as said below
- mode_ids: int32 [16], replicated, may hold values from 0 to 15, each once
Outputs:
- new_conformation: float32 [16, 6, 512, 4096], P('mode', None, 'pencil')
- spectral_stress: float32 [6, 4096, 512], P(None, ('mode', 'pencil'))
The draws below stay inside these ranges and needn't reach their ends.
Inputs may be any that keep to these rules, and one draw needn't show every extreme that they name: `counts`: some slot takes exactly 12 substeps and some slot exactly 1. `mode_ids`: each of the 16 mode indices is held by exactly one slot. `conformation`: at every point and slot the diagonal components lie in 0.5 to 3 and each off-diagonal component is at most 0.3 times the square root of the product of its two diagonal components in magnitude.
All inputs are finite; a program needn't handle non-finite values.
Results may differ from the reference program's by a relative error of at most 0.0003.
Values sent between devices are 32-bit elements; how exact they have to be, the bound alone decides.
No kernel may reach another device: no remote copies, remote signals or barrier semaphores. Data moves between devices by JAX's collectives and lax.ppermute only.
A program may use at most 128 MiB of HBM per device.

```python
import math
import jax
import jax.numpy as jnp
from jax import lax

NZ = 512
SUBSTEPS_MAX = 12
MODES = 16
COLS = 4096


def draw_conformation(key, part):
    key = jax.random.fold_in(key, 11)
    diag_key, couple_key = jax.random.split(key)
    field_shape = (MODES, 3, NZ, COLS)
    diagonal = jnp.exp(jax.random.uniform(diag_key, field_shape, jnp.float32, math.log(0.5), math.log(3.0)))
    coupling = 0.3 * jnp.tanh(jax.random.normal(couple_key, field_shape, jnp.float32))
    diag_xx, diag_yy, diag_zz = (diagonal[:, 0], diagonal[:, 1], diagonal[:, 2])
    return jnp.stack([diag_xx, coupling[:, 0] * jnp.sqrt(diag_xx * diag_yy), coupling[:, 1] * jnp.sqrt(diag_xx * diag_zz), diag_yy, coupling[:, 2] * jnp.sqrt(diag_yy * diag_zz), diag_zz], axis=1)


def draw_counts(key, part):
    key = jax.random.fold_in(key, 5)
    base_key, order_key = jax.random.split(key)
    substeps = jax.random.randint(base_key, (MODES,), 1, SUBSTEPS_MAX + 1, dtype=jnp.int32)
    ordering = jax.random.permutation(order_key, MODES)
    substeps = substeps.at[ordering[0]].set(SUBSTEPS_MAX)
    return substeps.at[ordering[1]].set(1)


def block_scale(own_key, extent, shards, smallest, largest):
    loudness, own = 1.0, jax.random.fold_in(own_key, 6)
    for dim, blocks in shards:
        draws = jnp.exp(jax.random.uniform(jax.random.fold_in(own, dim), (blocks,), jnp.float32, smallest / len(shards), largest / len(shards)))
        loudness = loudness * jnp.repeat(draws, extent[dim] // blocks).reshape([-1 if axis == dim else 1 for axis in range(len(extent))])
    return loudness


def setup_inputs(seed: int = 0) -> dict:
    splits = jax.random.split(jax.random.key(seed), 5)
    conformation = draw_conformation(jax.random.fold_in(splits[4], 71), 0)
    velocity_grad = jnp.clip(jax.random.uniform(splits[1], (8, NZ, COLS), jnp.float32, -1.0, 1.0) * block_scale(splits[1], (8, NZ, COLS), ((1, 32),), -0.4, 0.0), -1.0, 1.0)
    counts = draw_counts(jax.random.fold_in(splits[4], 71), 0)
    mode_ids = jax.random.permutation(splits[3], MODES).astype(jnp.int32)
    return {"conformation": conformation, "velocity_grad": velocity_grad, "counts": counts, "mode_ids": mode_ids}


step_time = 0.25
extension = 900.0

def transform_table(points_count):
    final_index = points_count - 1
    position = jnp.arange(points_count, dtype=jnp.int32)
    product = position[:, None] * position[None, :] % (2 * final_index)
    angles = jnp.pi * product.astype(jnp.float32) / final_index
    edge_weights = jnp.where((position == 0) | (position == final_index), math.sqrt(0.5), 1.0).astype(jnp.float32)
    return math.sqrt(2.0 / final_index) * edge_weights[:, None] * edge_weights[None, :] * jnp.cos(angles)

def diagonal_unit():
    return jnp.array([1.0, 0.0, 0.0, 1.0, 0.0, 1.0], dtype=jnp.float32).reshape(6, 1, 1)

def stretching(tensor, gradient):
    grad_xx, grad_xy, grad_xz = (gradient[0], gradient[1], gradient[2])
    grad_yx, grad_yy, grad_yz = (gradient[3], gradient[4], gradient[5])
    grad_zx, grad_zy = (gradient[6], gradient[7])
    grad_zz = -(grad_xx + grad_yy)
    conf_xx, conf_xy, conf_xz = (tensor[0], tensor[1], tensor[2])
    conf_yy, conf_yz, conf_zz = (tensor[3], tensor[4], tensor[5])
    prod_xx = grad_xx * conf_xx + grad_xy * conf_xy + grad_xz * conf_xz
    prod_xy = grad_xx * conf_xy + grad_xy * conf_yy + grad_xz * conf_yz
    prod_xz = grad_xx * conf_xz + grad_xy * conf_yz + grad_xz * conf_zz
    prod_yx = grad_yx * conf_xx + grad_yy * conf_xy + grad_yz * conf_xz
    prod_yy = grad_yx * conf_xy + grad_yy * conf_yy + grad_yz * conf_yz
    prod_yz = grad_yx * conf_xz + grad_yy * conf_yz + grad_yz * conf_zz
    prod_zx = grad_zx * conf_xx + grad_zy * conf_xy + grad_zz * conf_xz
    prod_zy = grad_zx * conf_xy + grad_zy * conf_yy + grad_zz * conf_yz
    prod_zz = grad_zx * conf_xz + grad_zy * conf_yz + grad_zz * conf_zz
    return jnp.stack([2.0 * prod_xx, prod_xy + prod_yx, prod_xz + prod_zx, 2.0 * prod_yy, prod_yz + prod_zy, 2.0 * prod_zz])

def peterlin(tensor):
    return (extension - 3.0) / (extension - (tensor[0] + tensor[3] + tensor[5]))

def substep(tensor, gradient, substep_time, inverse_tau):
    stretched = stretching(tensor, gradient)
    numerator = tensor + substep_time * stretched + substep_time * inverse_tau * diagonal_unit()
    return numerator / (1.0 + substep_time * inverse_tau * peterlin(tensor))

def reference(conformation, velocity_grad, counts, mode_ids):

    def advance(running, inputs):
        tensor, substeps, mode_index = inputs
        inverse_tau = ((mode_index + 1) * (mode_index + 1)).astype(jnp.float32)
        substep_time = step_time / substeps.astype(jnp.float32)

        def apply(step_index, current):
            moved = substep(current, velocity_grad, substep_time, inverse_tau)
            return jnp.where(step_index < substeps, moved, current)
        tensor = lax.fori_loop(0, SUBSTEPS_MAX, apply, tensor)
        running = running + inverse_tau / MODES * (peterlin(tensor) * tensor - diagonal_unit())
        return (running, tensor)
    initial = jnp.zeros((6, NZ, COLS), jnp.float32)
    stress, updated = lax.scan(advance, initial, (conformation, counts, mode_ids))
    spectral = jnp.einsum('czp,kz->cpk', stress, transform_table(NZ), precision=lax.Precision.HIGHEST)
    return (updated, spectral)
```

```python
import math

import jax
import jax.numpy as jnp
import ml_dtypes
import numpy as np
from jax import lax
from jax.experimental import pallas as pl
from jax.experimental.pallas import tpu as pltpu
from jax.sharding import PartitionSpec as P

step_time = 0.25
extension = 900.0
spring = extension - 3.0
F32 = jnp.float32
WIDTH = 512


def transform_table(points_count):
    final_index = points_count - 1
    position = np.arange(points_count)
    product = position[:, None] * position[None, :] % (2 * final_index)
    edge = np.where((position == 0) | (position == final_index), math.sqrt(0.5), 1.0)
    return math.sqrt(2.0 / final_index) * edge[:, None] * edge[None, :] * np.cos(np.pi * product / final_index)


def split_table(points_count):
    table = transform_table(points_count)
    high = table.astype(ml_dtypes.bfloat16)
    low = (table - high.astype(np.float64)).astype(ml_dtypes.bfloat16)
    return high, low


def advance_kernel(modes_total, first_ref, counts_ref, ids_ref, conf_ref, grad_ref, new_ref, stress_ref):
    slots, _, rows, columns = conf_ref.shape
    width = min(WIDTH, columns)
    across = columns // width

    def tile(index, carry):
        row = pl.multiple_of(index // across * 8, 8)
        column = pl.multiple_of(index % across * width, width)
        here = (pl.ds(row, 8), pl.ds(column, width))
        total = None
        for slot in range(slots):
            substeps = counts_ref[first_ref[0] + slot]
            order = ids_ref[first_ref[0] + slot] + 1
            rate = (order * order).astype(F32)
            step = step_time / jnp.full((8, 128), substeps.astype(F32), F32)
            step = jnp.concatenate([step] * (width // 128), axis=1)
            relax = step * rate
            xx, xy, xz, yx, yy, yz, zx, zy = (grad_ref[(i,) + here] * step for i in range(8))
            zz = -(xx + yy)
            both_xy, both_xz, both_yz = 1.0 - zz, 1.0 - yy, 1.0 - xx
            twice_xx, twice_yy, twice_zz = 1.0 + 2.0 * xx, 1.0 + 2.0 * yy, 1.0 + 2.0 * zz
            twice_xy, twice_xz, twice_yx = 2.0 * xy, 2.0 * xz, 2.0 * yx
            twice_yz, twice_zx, twice_zy = 2.0 * yz, 2.0 * zx, 2.0 * zy
            pull = relax * spring

            def substep(_, parts):
                cxx, cxy, cxz, cyy, cyz, czz = parts
                room = extension - (cxx + cyy + czz)
                scale = room * (1.0 / (room + pull))
                nxx = twice_xx * cxx + twice_xy * cxy + twice_xz * cxz + relax
                nyy = twice_yx * cxy + twice_yy * cyy + twice_yz * cyz + relax
                nzz = twice_zx * cxz + twice_zy * cyz + twice_zz * czz + relax
                nxy = both_xy * cxy + xy * cyy + xz * cyz + yx * cxx + yz * cxz
                nxz = both_xz * cxz + xy * cyz + xz * czz + zx * cxx + zy * cxy
                nyz = both_yz * cyz + yx * cxz + yz * czz + zx * cxy + zy * cyy
                return tuple(n * scale for n in (nxx, nxy, nxz, nyy, nyz, nzz))

            parts = tuple(conf_ref[(slot, i) + here] for i in range(6))
            parts = lax.fori_loop(0, substeps, substep, parts)
            for i in range(6):
                new_ref[(slot, i) + here] = parts[i]
            weight = rate / modes_total
            factor = weight * spring / (extension - (parts[0] + parts[3] + parts[5]))
            terms = [factor * part - (weight if i in (0, 3, 5) else 0.0) for i, part in enumerate(parts)]
            total = terms if total is None else [a + b for a, b in zip(total, terms)]
        for i in range(6):
            stress_ref[(0, i) + here] = total[i]
        return carry

    lax.fori_loop(0, rows // 8 * across, tile, 0)


def advance(first, counts, ids, conformation, gradient, blocks):
    slots, _, rows, columns = conformation.shape
    block = columns // blocks
    return pl.pallas_call(
        lambda *refs: advance_kernel(float(counts.shape[0]), *refs),
        grid_spec=pltpu.PrefetchScalarGridSpec(
            num_scalar_prefetch=3,
            grid=(blocks,),
            in_specs=[
                pl.BlockSpec((slots, 6, rows, block), lambda i, *_: (0, 0, 0, i)),
                pl.BlockSpec((8, rows, block), lambda i, *_: (0, 0, i)),
            ],
            out_specs=[
                pl.BlockSpec((slots, 6, rows, block), lambda i, *_: (0, 0, 0, i)),
                pl.BlockSpec((1, 6, rows, block), lambda i, *_: (i, 0, 0, 0)),
            ],
        ),
        out_shape=[
            jax.ShapeDtypeStruct(conformation.shape, F32),
            jax.ShapeDtypeStruct((blocks, 6, rows, block), F32),
        ],
        compiler_params=pltpu.CompilerParams(vmem_limit_bytes=12 * 2**20),
        cost_estimate=pl.CostEstimate(flops=65536 * 60 * 13 * 2, bytes_accessed=10 * 2**20, transcendentals=0),
        name="advance",
    )(first, counts, ids, conformation, gradient)


def pack_kernel(share, parts_ref, out_ref):
    sources, comps, rows, block = parts_ref.shape
    group = 128 // share
    lane = lax.broadcasted_iota(jnp.int32, (8, 128), 1) // share
    for row in range(0, rows, 8):
        for tile in range(0, block, 128):
            sums = []
            for comp in range(comps):
                total = parts_ref[0, comp, row : row + 8, tile : tile + 128]
                for source in range(1, sources):
                    total = total + parts_ref[source, comp, row : row + 8, tile : tile + 128]
                sums.append(total)
            for member in range(group):
                packed = jnp.zeros((8, 128), F32)
                for comp in range(comps):
                    shift = (comp - member) % group * share
                    moved = pltpu.roll(sums[comp], shift, 1) if shift else sums[comp]
                    packed = jnp.where(lane == comp, moved, packed)
                out_ref[tile // share + member, row : row + 8, :] = packed


def pack(parts, pencils):
    sources, comps, rows, block = parts.shape
    share = block // pencils
    return pl.pallas_call(
        lambda *refs: pack_kernel(share, *refs),
        out_shape=jax.ShapeDtypeStruct((pencils, rows, 128), F32),
        compiler_params=pltpu.CompilerParams(vmem_limit_bytes=12 * 2**20),
        cost_estimate=pl.CostEstimate(flops=400 * 1024, bytes_accessed=2**21, transcendentals=0),
        name="pack",
    )(parts)


def transform_kernel(comps, share, values_ref, high_ref, low_ref, out_ref):
    values = values_ref[...]
    high = values.astype(jnp.bfloat16)
    low = (values - high.astype(F32)).astype(jnp.bfloat16)

    def product(table, part):
        return jnp.dot(table, part, preferred_element_type=F32)

    result = product(high_ref[...], high) + (product(high_ref[...], low) + product(low_ref[...], high))
    result = result.T
    for comp in range(comps):
        out_ref[comp] = result[comp * share : (comp + 1) * share]


def transform(values, comps, share):
    points = values.shape[0]
    high, low = split_table(points)
    return pl.pallas_call(
        lambda *refs: transform_kernel(comps, share, *refs),
        out_shape=jax.ShapeDtypeStruct((comps, share, points), F32),
        compiler_params=pltpu.CompilerParams(vmem_limit_bytes=12 * 2**20),
        cost_estimate=pl.CostEstimate(flops=2 * 3 * 128 * 512 * 512, bytes_accessed=2**21, transcendentals=0),
        name="transform",
    )(values, high, low)


def per_device(conformation, gradient, counts, mode_ids):
    slots, comps, rows, columns = conformation.shape
    modes, pencils = lax.axis_size("mode"), lax.axis_size("pencil")
    first = (lax.axis_index("mode") * slots).astype(jnp.int32).reshape(1)
    new_conformation, partial = advance(first, counts, mode_ids, conformation, gradient, modes)
    parts = lax.all_to_all(partial, "mode", split_axis=0, concat_axis=0, tiled=True)
    packed = pack(parts, pencils)
    planes = lax.all_to_all(packed, "pencil", split_axis=0, concat_axis=0, tiled=True)
    share = columns // modes // pencils
    return new_conformation, transform(planes.reshape(rows * pencils, 128), comps, share)


def solution(mesh):
    in_specs = (P("mode", None, "pencil", None), P(None, "pencil", None), P(), P())
    out_specs = (P("mode", None, "pencil", None), P(None, ("mode", "pencil"), None))
    return jax.shard_map(
        per_device, mesh=mesh, in_specs=in_specs, out_specs=out_specs, check_vma=False
    )
```

```python
import functools
import math

import jax
import jax.numpy as jnp
import ml_dtypes
import numpy as np
from jax import lax
from jax.experimental import pallas as pl
from jax.experimental.pallas import tpu as pltpu
from jax.sharding import PartitionSpec as P

step_time = 0.25
extension = 900.0
spring = extension - 3.0
F32 = jnp.float32
WIDTH = 512
UNROLL = 2
LIMIT = 16 * 2**20
AHEAD = 4
FIRST_LIMIT = 52 * 2**20


def transform_table(points_count):
    final_index = points_count - 1
    position = np.arange(points_count)
    product = position[:, None] * position[None, :] % (2 * final_index)
    edge = np.where((position == 0) | (position == final_index), math.sqrt(0.5), 1.0)
    return math.sqrt(2.0 / final_index) * edge[:, None] * edge[None, :] * np.cos(np.pi * product / final_index)


def split_table(points_count):
    table = transform_table(points_count)
    high = table.astype(ml_dtypes.bfloat16)
    low = (table - high.astype(np.float64)).astype(ml_dtypes.bfloat16)
    return high, low


def offsets(modes, runs):
    rings = modes // runs
    steps = [(run, ring) for run in range(runs) for ring in range(rings)]
    return sorted(steps, key=lambda s: (-min(s[1], rings - s[1]) - s[0], -s[0], s[1]))


def partner(mode, offset, modes, runs):
    run, ring = offset
    return (mode // runs + ring) % (modes // runs) * runs + (mode % runs + run) % runs


def wide(value, width):
    return jnp.concatenate([value] * (width // value.shape[1]), axis=1)


def advance_block(modes_total, facts_ref, conf_ref, grad_ref, new_ref, stress_ref):
    slots, _, rows, columns = new_ref.shape
    width = min(WIDTH, columns)
    across = columns // width

    substeps = [jnp.max(facts_ref[slot]) for slot in range(slots)]

    def tile(index, carry):
        row = pl.multiple_of(index // across * 8, 8)
        column = pl.multiple_of(index % across * width, width)
        here = (pl.ds(row, 8), pl.ds(column, width))
        total = None
        for slot in range(slots):
            rate = wide(facts_ref[slots + slot].astype(F32), width)
            step = step_time / wide(facts_ref[slot].astype(F32), width)
            relax = step * rate
            xx, xy, xz, yx, yy, yz, zx, zy = (grad_ref[(i,) + here] * step for i in range(8))
            zz = -(xx + yy)
            both_xy, both_xz, both_yz = 1.0 - zz, 1.0 - yy, 1.0 - xx
            twice_xx, twice_yy, twice_zz = 1.0 + 2.0 * xx, 1.0 + 2.0 * yy, 1.0 + 2.0 * zz
            twice_xy, twice_xz, twice_yx = 2.0 * xy, 2.0 * xz, 2.0 * yx
            twice_yz, twice_zx, twice_zy = 2.0 * yz, 2.0 * zx, 2.0 * zy
            pull = relax * spring

            def substep(_, parts):
                cxx, cxy, cxz, cyy, cyz, czz = parts
                room = extension - (cxx + cyy + czz)
                scale = room * (1.0 / (room + pull))
                nxx = twice_xx * cxx + twice_xy * cxy + twice_xz * cxz + relax
                nyy = twice_yx * cxy + twice_yy * cyy + twice_yz * cyz + relax
                nzz = twice_zx * cxz + twice_zy * cyz + twice_zz * czz + relax
                nxy = both_xy * cxy + xy * cyy + xz * cyz + yx * cxx + yz * cxz
                nxz = both_xz * cxz + xy * cyz + xz * czz + zx * cxx + zy * cxy
                nyz = both_yz * cyz + yx * cxz + yz * czz + zx * cxy + zy * cyy
                return tuple(n * scale for n in (nxx, nxy, nxz, nyy, nyz, nzz))

            def several(_, parts):
                for _ in range(UNROLL):
                    parts = substep(_, parts)
                return parts

            parts = tuple(conf_ref[(slot, i) + here] for i in range(6))
            parts = lax.fori_loop(0, substeps[slot] // UNROLL, several, parts)
            parts = lax.fori_loop(0, substeps[slot] % UNROLL, substep, parts)
            for i in range(6):
                new_ref[(slot, i) + here] = parts[i]
            weight = rate / modes_total
            factor = weight * spring / (extension - (parts[0] + parts[3] + parts[5]))
            terms = [factor * part - (weight if i in (0, 3, 5) else 0.0) for i, part in enumerate(parts)]
            total = terms if total is None else [a + b for a, b in zip(total, terms)]
        for i in range(6):
            stress_ref[(i,) + here] = total[i]
        return carry

    lax.fori_loop(0, rows // 8 * across, tile, 0)


def columns_of(target, columns):
    return pl.ds(pl.multiple_of(target * columns, columns), columns)


def fetch(target, conf_hbm, grad_hbm, conf_ref, grad_ref, sems):
    span = columns_of(target, conf_ref.shape[3])
    return [
        pltpu.make_async_copy(conf_hbm.at[:, :, :, span], conf_ref, sems.at[0]),
        pltpu.make_async_copy(grad_hbm.at[:, :, span], grad_ref, sems.at[1]),
    ]


def start(copies):
    for copy in copies:
        copy.start()


def wait(copies):
    for copy in copies:
        copy.wait()


def first_kernel(steps, modes, runs, mode_ref, counts_hbm, ids_hbm, conf_hbm, grad_hbm, stress_ref, new_ref,
                 next_conf_ref, next_grad_ref, facts_ref, conf_ref, grad_ref, counts_ref, ids_ref, sems):
    mode = mode_ref[0]
    slots = new_ref.shape[0]
    small = [
        pltpu.make_async_copy(counts_hbm, counts_ref, sems.at[4]),
        pltpu.make_async_copy(ids_hbm, ids_ref, sems.at[5]),
    ]
    own = fetch(partner(mode, steps[0], modes, runs), conf_hbm, grad_hbm, conf_ref, grad_ref, sems.at[0:2])
    following = fetch(partner(mode, steps[1], modes, runs), conf_hbm, grad_hbm, next_conf_ref, next_grad_ref, sems.at[2:4])
    start(small + own + following)
    wait(small)
    for slot in range(slots):
        order = ids_ref[mode * slots + slot] + 1
        facts_ref[slot] = jnp.full((8, 128), counts_ref[mode * slots + slot], jnp.int32)
        facts_ref[slots + slot] = jnp.full((8, 128), order * order, jnp.int32)
    wait(own)
    advance_block(float(counts_hbm.shape[0]), facts_ref, conf_ref, grad_ref, new_ref, stress_ref)
    wait(following)


def middle_kernel(step, modes, runs, modes_total, mode_ref, facts_ref, conf_hbm, grad_hbm, conf_ref, grad_ref, *refs):
    stress_ref, new_ref, next_conf_ref, next_grad_ref, sems = refs[-5:]
    following = fetch(partner(mode_ref[0], step, modes, runs), conf_hbm, grad_hbm, next_conf_ref, next_grad_ref, sems)
    start(following)
    advance_block(modes_total, facts_ref, conf_ref, grad_ref, new_ref, stress_ref)
    wait(following)


def last_kernel(steps, modes, runs, modes_total, mode_ref, facts_ref, conf_ref, grad_ref, *refs):
    done, (stress_ref, out_hbm, new_ref, sems) = refs[: len(steps) - 1], refs[len(steps) - 1 :]
    mode = mode_ref[0]
    copies = []
    for k, (step, ref) in enumerate(zip(steps, list(done) + [new_ref])):
        span = columns_of(partner(mode, step, modes, runs), new_ref.shape[3])
        copies.append(pltpu.make_async_copy(ref, out_hbm.at[:, :, :, span], sems.at[k]))
    start(copies[:-1])
    advance_block(modes_total, facts_ref, conf_ref, grad_ref, new_ref, stress_ref)
    copies[-1].start()
    wait(copies)


def advance(mode, counts, ids, conformation, gradient, modes, runs, send):
    slots, comps, rows, columns = conformation.shape
    block = columns // modes
    steps = offsets(modes, runs)
    total = float(counts.shape[0])
    smem, vmem, hbm = (pl.BlockSpec(memory_space=s) for s in (pltpu.SMEM, pltpu.VMEM, pltpu.HBM))
    stress = jax.ShapeDtypeStruct((comps, rows, block), F32)
    new = pltpu.VMEM((slots, comps, rows, block), F32)
    grad = pltpu.VMEM((8, rows, block), F32)
    dma = pltpu.SemaphoreType.DMA
    cost = pl.CostEstimate(flops=1024, bytes_accessed=1024, transcendentals=0)
    counts, ids, conformation, gradient = (pltpu.with_memory_space_constraint(x, pltpu.HBM) for x in (counts, ids, conformation, gradient))
    out = pl.pallas_call(
        lambda *refs: first_kernel(steps, modes, runs, *refs),
        in_specs=[smem] + [hbm] * 4,
        out_specs=[vmem] * 5,
        out_shape=[stress, new, new, grad, pltpu.VMEM((2 * slots, 8, 128), jnp.int32)],
        scratch_shapes=[new, grad, pltpu.SMEM(counts.shape, jnp.int32), pltpu.SMEM(ids.shape, jnp.int32), dma((6,))],
        compiler_params=pltpu.CompilerParams(vmem_limit_bytes=FIRST_LIMIT),
        cost_estimate=cost,
        name="advance_first",
    )(mode, counts, ids, conformation, gradient)
    parts, news, held, facts = [send(steps[0], out[0])], [out[1]], out[2:4], out[4]
    for k in range(1, modes - 1):
        order = [news[-1]] + parts[max(k - AHEAD, 0) : max(k - AHEAD + 1, 0)]
        out = pl.pallas_call(
            lambda *refs, step=steps[k + 1]: middle_kernel(step, modes, runs, total, *refs),
            in_specs=[smem, vmem, hbm, hbm] + [vmem] * (2 + len(order)),
            out_specs=[vmem] * 4,
            out_shape=[stress, new, new, grad],
            scratch_shapes=[dma((2,))],
            compiler_params=pltpu.CompilerParams(vmem_limit_bytes=LIMIT),
            cost_estimate=cost,
            name="advance_middle",
        )(mode, facts, conformation, gradient, *held, *order)
        parts.append(send(steps[k], out[0]))
        news.append(out[1])
        held = out[2:4]
    out = pl.pallas_call(
        lambda *refs: last_kernel(steps, modes, runs, total, *refs),
        in_specs=[smem, vmem] + [vmem] * (2 + len(news)),
        out_specs=[vmem, hbm],
        out_shape=[stress, jax.ShapeDtypeStruct(conformation.shape, F32)],
        scratch_shapes=[new, dma((modes,))],
        compiler_params=pltpu.CompilerParams(vmem_limit_bytes=LIMIT),
        cost_estimate=cost,
        name="advance_last",
    )(mode, facts, *held, *news)
    return parts + [send(steps[-1], out[0])], out[1]


def pack_kernel(share, *refs):
    parts_refs, out_ref = refs[:-1], refs[-1]
    comps, rows, block = parts_refs[0].shape
    group = 128 // share
    lane = lax.broadcasted_iota(jnp.int32, (8, 128), 1) // share
    for row in range(0, rows, 8):
        for tile in range(0, block, 128):
            sums = []
            for comp in range(comps):
                sums.append(sum(ref[comp, row : row + 8, tile : tile + 128] for ref in parts_refs))
            for member in range(group):
                packed = jnp.zeros((8, 128), F32)
                for comp in range(comps):
                    shift = (comp - member) % group * share
                    moved = pltpu.roll(sums[comp], shift, 1) if shift else sums[comp]
                    packed = jnp.where(lane == comp, moved, packed)
                out_ref[tile // share + member, row : row + 8, :] = packed


def pack(parts, pencils):
    comps, rows, block = parts[0].shape
    share = block // pencils
    return pl.pallas_call(
        lambda *refs: pack_kernel(share, *refs),
        out_shape=jax.ShapeDtypeStruct((pencils, rows, 128), F32),
        compiler_params=pltpu.CompilerParams(vmem_limit_bytes=12 * 2**20),
        cost_estimate=pl.CostEstimate(flops=400 * 1024, bytes_accessed=2**21, transcendentals=0),
        name="pack",
    )(*parts)


def transform_kernel(comps, share, values_ref, high_ref, low_ref, out_ref):
    values = values_ref[...]
    high = values.astype(jnp.bfloat16)
    low = (values - high.astype(F32)).astype(jnp.bfloat16)

    def product(table, part):
        return jnp.dot(table, part, preferred_element_type=F32)

    result = product(high_ref[...], high) + (product(high_ref[...], low) + product(low_ref[...], high))
    result = result.T
    for comp in range(comps):
        out_ref[comp] = result[comp * share : (comp + 1) * share]


def transform(values, comps, share):
    points = values.shape[0]
    high, low = split_table(points)
    return pl.pallas_call(
        lambda *refs: transform_kernel(comps, share, *refs),
        out_shape=jax.ShapeDtypeStruct((comps, share, points), F32),
        compiler_params=pltpu.CompilerParams(vmem_limit_bytes=12 * 2**20),
        cost_estimate=pl.CostEstimate(flops=2 * 3 * 128 * 512 * 512, bytes_accessed=2**21, transcendentals=0),
        name="transform",
    )(values, high, low)


def per_device(runs, conformation, gradient, counts, mode_ids):
    slots, comps, rows, columns = conformation.shape
    modes, pencils = lax.axis_size("mode"), lax.axis_size("pencil")
    mode = lax.axis_index("mode").astype(jnp.int32).reshape(1)

    def send(step, value):
        if step == (0, 0):
            return value
        return lax.ppermute(value, "mode", [(m, partner(m, step, modes, runs)) for m in range(modes)])

    parts, new_conformation = advance(mode, counts, mode_ids, conformation, gradient, modes, runs, send)
    packed = pack(parts, pencils)
    planes = lax.all_to_all(packed, "pencil", split_axis=0, concat_axis=0, tiled=True)
    share = columns // modes // pencils
    return new_conformation, transform(planes.reshape(rows * pencils, 128), comps, share)


def solution(mesh):
    in_specs = (P("mode", None, "pencil", None), P(None, "pencil", None), P(), P())
    out_specs = (P("mode", None, "pencil", None), P(None, ("mode", "pencil"), None))
    return jax.shard_map(
        functools.partial(per_device, 2), mesh=mesh, in_specs=in_specs, out_specs=out_specs, check_vma=False
    )
```

```python
import functools
import math

import jax
import jax.numpy as jnp
import ml_dtypes
import numpy as np
from jax import lax
from jax.experimental import pallas as pl
from jax.experimental.pallas import tpu as pltpu
from jax.sharding import PartitionSpec as P

step_time = 0.25
extension = 900.0
spring = extension - 3.0
F32 = jnp.float32
WIDTH = 512
UNROLL = 2
LIMIT = 16 * 2**20
AHEAD = 6
FIRST_LIMIT = 52 * 2**20


def transform_table(points_count):
    final_index = points_count - 1
    position = np.arange(points_count)
    product = position[:, None] * position[None, :] % (2 * final_index)
    edge = np.where((position == 0) | (position == final_index), math.sqrt(0.5), 1.0)
    return math.sqrt(2.0 / final_index) * edge[:, None] * edge[None, :] * np.cos(np.pi * product / final_index)


def split_table(points_count):
    table = transform_table(points_count)
    high = table.astype(ml_dtypes.bfloat16)
    low = (table - high.astype(np.float64)).astype(ml_dtypes.bfloat16)
    return high, low


def offsets(modes, runs):
    rings = modes // runs
    steps = [(run, ring) for run in range(runs) for ring in range(rings)]
    return sorted(steps, key=lambda s: (-min(s[1], rings - s[1]) - s[0], -s[0], s[1]))


def partner(mode, offset, modes, runs):
    run, ring = offset
    return (mode // runs + ring) % (modes // runs) * runs + (mode % runs + run) % runs


def wide(value, width):
    return jnp.concatenate([value] * (width // value.shape[1]), axis=1)


def advance_block(modes_total, facts_ref, conf_ref, grad_ref, new_ref, stress_ref):
    slots, _, rows, columns = new_ref.shape
    width = min(WIDTH, columns)
    across = columns // width

    substeps = [jnp.max(facts_ref[slot]) for slot in range(slots)]

    def tile(index, carry):
        row = pl.multiple_of(index // across * 8, 8)
        column = pl.multiple_of(index % across * width, width)
        here = (pl.ds(row, 8), pl.ds(column, width))
        total = None
        for slot in range(slots):
            rate = wide(facts_ref[slots + slot].astype(F32), width)
            step = step_time / wide(facts_ref[slot].astype(F32), width)
            relax = step * rate
            xx, xy, xz, yx, yy, yz, zx, zy = (grad_ref[(i,) + here] * step for i in range(8))
            zz = -(xx + yy)
            both_xy, both_xz, both_yz = 1.0 - zz, 1.0 - yy, 1.0 - xx
            twice_xx, twice_yy, twice_zz = 1.0 + 2.0 * xx, 1.0 + 2.0 * yy, 1.0 + 2.0 * zz
            twice_xy, twice_xz, twice_yx = 2.0 * xy, 2.0 * xz, 2.0 * yx
            twice_yz, twice_zx, twice_zy = 2.0 * yz, 2.0 * zx, 2.0 * zy
            pull = relax * spring

            def substep(_, parts):
                cxx, cxy, cxz, cyy, cyz, czz = parts
                room = extension - (cxx + cyy + czz)
                scale = room * (1.0 / (room + pull))
                nxx = twice_xx * cxx + twice_xy * cxy + twice_xz * cxz + relax
                nyy = twice_yx * cxy + twice_yy * cyy + twice_yz * cyz + relax
                nzz = twice_zx * cxz + twice_zy * cyz + twice_zz * czz + relax
                nxy = both_xy * cxy + xy * cyy + xz * cyz + yx * cxx + yz * cxz
                nxz = both_xz * cxz + xy * cyz + xz * czz + zx * cxx + zy * cxy
                nyz = both_yz * cyz + yx * cxz + yz * czz + zx * cxy + zy * cyy
                return tuple(n * scale for n in (nxx, nxy, nxz, nyy, nyz, nzz))

            def several(_, parts):
                for _ in range(UNROLL):
                    parts = substep(_, parts)
                return parts

            parts = tuple(conf_ref[(slot, i) + here] for i in range(6))
            parts = lax.fori_loop(0, substeps[slot] // UNROLL, several, parts)
            parts = lax.fori_loop(0, substeps[slot] % UNROLL, substep, parts)
            for i in range(6):
                new_ref[(slot, i) + here] = parts[i]
            weight = rate / modes_total
            factor = weight * spring / (extension - (parts[0] + parts[3] + parts[5]))
            terms = [factor * part - (weight if i in (0, 3, 5) else 0.0) for i, part in enumerate(parts)]
            total = terms if total is None else [a + b for a, b in zip(total, terms)]
        for i in range(6):
            stress_ref[(i,) + here] = total[i]
        return carry

    lax.fori_loop(0, rows // 8 * across, tile, 0)


def columns_of(target, columns):
    return pl.ds(pl.multiple_of(target * columns, columns), columns)


def fetch(target, conf_hbm, grad_hbm, conf_ref, grad_ref, sems):
    span = columns_of(target, conf_ref.shape[3])
    return [
        pltpu.make_async_copy(conf_hbm.at[:, :, :, span], conf_ref, sems.at[0]),
        pltpu.make_async_copy(grad_hbm.at[:, :, span], grad_ref, sems.at[1]),
    ]


def start(copies):
    for copy in copies:
        copy.start()


def wait(copies):
    for copy in copies:
        copy.wait()


def first_kernel(steps, modes, runs, mode_ref, counts_hbm, ids_hbm, conf_hbm, grad_hbm, stress_ref, new_ref,
                 next_conf_ref, next_grad_ref, facts_ref, conf_ref, grad_ref, counts_ref, ids_ref, sems):
    mode = mode_ref[0]
    slots = new_ref.shape[0]
    small = [
        pltpu.make_async_copy(counts_hbm, counts_ref, sems.at[4]),
        pltpu.make_async_copy(ids_hbm, ids_ref, sems.at[5]),
    ]
    own = fetch(partner(mode, steps[0], modes, runs), conf_hbm, grad_hbm, conf_ref, grad_ref, sems.at[0:2])
    following = fetch(partner(mode, steps[1], modes, runs), conf_hbm, grad_hbm, next_conf_ref, next_grad_ref, sems.at[2:4])
    start(small + own + following)
    wait(small)
    for slot in range(slots):
        order = ids_ref[mode * slots + slot] + 1
        facts_ref[slot] = jnp.full((8, 128), counts_ref[mode * slots + slot], jnp.int32)
        facts_ref[slots + slot] = jnp.full((8, 128), order * order, jnp.int32)
    wait(own)
    advance_block(float(counts_hbm.shape[0]), facts_ref, conf_ref, grad_ref, new_ref, stress_ref)
    wait(following)


def middle_kernel(step, modes, runs, modes_total, mode_ref, facts_ref, conf_hbm, grad_hbm, conf_ref, grad_ref, *refs):
    stress_ref, new_ref, next_conf_ref, next_grad_ref, sems = refs[-5:]
    following = fetch(partner(mode_ref[0], step, modes, runs), conf_hbm, grad_hbm, next_conf_ref, next_grad_ref, sems)
    start(following)
    advance_block(modes_total, facts_ref, conf_ref, grad_ref, new_ref, stress_ref)
    wait(following)


def last_kernel(steps, modes, runs, modes_total, mode_ref, facts_ref, conf_ref, grad_ref, *refs):
    done, (stress_ref, out_hbm, new_ref, sems) = refs[: len(steps) - 1], refs[len(steps) - 1 :]
    mode = mode_ref[0]
    copies = []
    for k, (step, ref) in enumerate(zip(steps, list(done) + [new_ref])):
        span = columns_of(partner(mode, step, modes, runs), new_ref.shape[3])
        copies.append(pltpu.make_async_copy(ref, out_hbm.at[:, :, :, span], sems.at[k]))
    start(copies[:-1])
    advance_block(modes_total, facts_ref, conf_ref, grad_ref, new_ref, stress_ref)
    copies[-1].start()
    wait(copies)


def advance(mode, counts, ids, conformation, gradient, modes, runs, send):
    slots, comps, rows, columns = conformation.shape
    block = columns // modes
    steps = offsets(modes, runs)
    total = float(counts.shape[0])
    smem, vmem, hbm = (pl.BlockSpec(memory_space=s) for s in (pltpu.SMEM, pltpu.VMEM, pltpu.HBM))
    stress = jax.ShapeDtypeStruct((comps, rows, block), F32)
    new = pltpu.VMEM((slots, comps, rows, block), F32)
    grad = pltpu.VMEM((8, rows, block), F32)
    dma = pltpu.SemaphoreType.DMA
    cost = pl.CostEstimate(flops=1024, bytes_accessed=1024, transcendentals=0)
    counts, ids, conformation, gradient = (pltpu.with_memory_space_constraint(x, pltpu.HBM) for x in (counts, ids, conformation, gradient))
    out = pl.pallas_call(
        lambda *refs: first_kernel(steps, modes, runs, *refs),
        in_specs=[smem] + [hbm] * 4,
        out_specs=[vmem] * 5,
        out_shape=[stress, new, new, grad, pltpu.VMEM((2 * slots, 8, 128), jnp.int32)],
        scratch_shapes=[new, grad, pltpu.SMEM(counts.shape, jnp.int32), pltpu.SMEM(ids.shape, jnp.int32), dma((6,))],
        compiler_params=pltpu.CompilerParams(vmem_limit_bytes=FIRST_LIMIT),
        cost_estimate=cost,
        name="advance_first",
    )(mode, counts, ids, conformation, gradient)
    parts, news, held, facts = [send(steps[0], out[0])], [out[1]], out[2:4], out[4]
    for k in range(1, modes - 1):
        order = [news[-1]] + parts[max(k - AHEAD, 0) : max(k - AHEAD + 1, 0)]
        out = pl.pallas_call(
            lambda *refs, step=steps[k + 1]: middle_kernel(step, modes, runs, total, *refs),
            in_specs=[smem, vmem, hbm, hbm] + [vmem] * (2 + len(order)),
            out_specs=[vmem] * 4,
            out_shape=[stress, new, new, grad],
            scratch_shapes=[dma((2,))],
            compiler_params=pltpu.CompilerParams(vmem_limit_bytes=LIMIT),
            cost_estimate=cost,
            name="advance_middle",
        )(mode, facts, conformation, gradient, *held, *order)
        parts.append(send(steps[k], out[0]))
        news.append(out[1])
        held = out[2:4]
    out = pl.pallas_call(
        lambda *refs: last_kernel(steps, modes, runs, total, *refs),
        in_specs=[smem, vmem] + [vmem] * (2 + len(news)),
        out_specs=[vmem, hbm],
        out_shape=[stress, jax.ShapeDtypeStruct(conformation.shape, F32)],
        scratch_shapes=[new, dma((modes,))],
        compiler_params=pltpu.CompilerParams(vmem_limit_bytes=LIMIT),
        cost_estimate=cost,
        name="advance_last",
    )(mode, facts, *held, *news)
    return parts + [send(steps[-1], out[0])], out[1]


def pack_kernel(share, *refs):
    parts_refs, out_ref = refs[:-1], refs[-1]
    comps, rows, block = parts_refs[0].shape
    group = 128 // share
    lane = lax.broadcasted_iota(jnp.int32, (8, 128), 1) // share
    for row in range(0, rows, 8):
        for tile in range(0, block, 128):
            sums = []
            for comp in range(comps):
                sums.append(sum(ref[comp, row : row + 8, tile : tile + 128] for ref in parts_refs))
            sums += [jnp.zeros((8, 128), F32)] * (group - comps)
            distance = 1
            while distance < group:
                low = lane & distance == 0
                for i in range(group):
                    if i & distance == 0:
                        first, second = sums[i], sums[i + distance]
                        sums[i] = jnp.where(low, first, pltpu.roll(second, distance * share, 1))
                        sums[i + distance] = jnp.where(low, pltpu.roll(first, 128 - distance * share, 1), second)
                distance *= 2
            for member in range(group):
                out_ref[tile // share + member, row : row + 8, :] = sums[member]


def pack(parts, pencils):
    comps, rows, block = parts[0].shape
    share = block // pencils
    return pl.pallas_call(
        lambda *refs: pack_kernel(share, *refs),
        out_shape=jax.ShapeDtypeStruct((pencils, rows, 128), F32),
        compiler_params=pltpu.CompilerParams(vmem_limit_bytes=12 * 2**20),
        cost_estimate=pl.CostEstimate(flops=400 * 1024, bytes_accessed=2**21, transcendentals=0),
        name="pack",
    )(*parts)


def transform_kernel(comps, share, values_ref, high_ref, low_ref, out_ref):
    values = values_ref[...]
    high = values.astype(jnp.bfloat16)
    low = (values - high.astype(F32)).astype(jnp.bfloat16)

    both = jnp.dot(high_ref[...], jnp.concatenate([high, low], axis=1), preferred_element_type=F32)
    cross = jnp.dot(low_ref[...], high, preferred_element_type=F32)
    width = values.shape[1]
    result = both[:, :width] + (both[:, width:] + cross)
    result = result.T
    for comp in range(comps):
        out_ref[comp] = result[comp * share : (comp + 1) * share]


def transform(values, comps, share):
    points = values.shape[0]
    high, low = split_table(points)
    return pl.pallas_call(
        lambda *refs: transform_kernel(comps, share, *refs),
        out_shape=jax.ShapeDtypeStruct((comps, share, points), F32),
        compiler_params=pltpu.CompilerParams(vmem_limit_bytes=12 * 2**20),
        cost_estimate=pl.CostEstimate(flops=2 * 3 * 128 * 512 * 512, bytes_accessed=2**21, transcendentals=0),
        name="transform",
    )(values, high, low)


def per_device(runs, conformation, gradient, counts, mode_ids):
    slots, comps, rows, columns = conformation.shape
    modes, pencils = lax.axis_size("mode"), lax.axis_size("pencil")
    mode = lax.axis_index("mode").astype(jnp.int32).reshape(1)

    def send(step, value):
        if step == (0, 0):
            return value
        return lax.ppermute(value, "mode", [(m, partner(m, step, modes, runs)) for m in range(modes)])

    parts, new_conformation = advance(mode, counts, mode_ids, conformation, gradient, modes, runs, send)
    packed = pack(parts, pencils)
    planes = lax.all_to_all(packed, "pencil", split_axis=0, concat_axis=0, tiled=True)
    share = columns // modes // pencils
    return new_conformation, transform(planes.reshape(rows * pencils, 128), comps, share)


def solution(mesh):
    in_specs = (P("mode", None, "pencil", None), P(None, "pencil", None), P(), P())
    out_specs = (P("mode", None, "pencil", None), P(None, ("mode", "pencil"), None))
    return jax.shard_map(
        functools.partial(per_device, 2), mesh=mesh, in_specs=in_specs, out_specs=out_specs, check_vma=False
    )
```

```python
import functools
import math

import jax
import jax.numpy as jnp
import ml_dtypes
import numpy as np
from jax import lax
from jax.experimental import pallas as pl
from jax.experimental.pallas import tpu as pltpu
from jax.sharding import PartitionSpec as P

step_time = 0.25
extension = 900.0
spring = extension - 3.0
F32 = jnp.float32
WIDTH = 512
UNROLL = 2
LIMIT = 16 * 2**20
FIRST_LIMIT = 52 * 2**20


def transform_table(points_count):
    final_index = points_count - 1
    position = np.arange(points_count)
    product = position[:, None] * position[None, :] % (2 * final_index)
    edge = np.where((position == 0) | (position == final_index), math.sqrt(0.5), 1.0)
    return math.sqrt(2.0 / final_index) * edge[:, None] * edge[None, :] * np.cos(np.pi * product / final_index)


def split_table(points_count):
    table = transform_table(points_count)
    high = table.astype(ml_dtypes.bfloat16)
    low = (table - high.astype(np.float64)).astype(ml_dtypes.bfloat16)
    return high, low


def plan(rings):
    assert rings == 4
    return [[(1, 2), (0, 2)], [(1, 3)], [(1, 0)], [(0, 3)], [(1, 1)], [(0, 1)], [(0, 0)]]


def partner(place, offset, modes, runs):
    mode, core = place // 2, place % 2
    rings = modes // runs
    ring = (mode // runs + rings + (1 - 2 * core) * offset[1]) % rings
    return ring * runs + (mode % runs + offset[0]) % runs


def wide(value, width):
    return jnp.concatenate([value] * (width // value.shape[1]), axis=1)


def advance_block(modes_total, facts_ref, conf_ref, grad_ref, new_ref, stress_ref, added_ref=None):
    slots, _, rows, columns = new_ref.shape
    width = min(WIDTH, columns)
    across = columns // width

    substeps = [jnp.max(facts_ref[slot]) for slot in range(slots)]

    def tile(index, carry):
        row = pl.multiple_of(index // across * 8, 8)
        column = pl.multiple_of(index % across * width, width)
        here = (pl.ds(row, 8), pl.ds(column, width))
        total = None
        for slot in range(slots):
            rate = wide(facts_ref[slots + slot].astype(F32), width)
            step = step_time / wide(facts_ref[slot].astype(F32), width)
            relax = step * rate
            xx, xy, xz, yx, yy, yz, zx, zy = (grad_ref[(i,) + here] * step for i in range(8))
            zz = -(xx + yy)
            both_xy, both_xz, both_yz = 1.0 - zz, 1.0 - yy, 1.0 - xx
            twice_xx, twice_yy, twice_zz = 1.0 + 2.0 * xx, 1.0 + 2.0 * yy, 1.0 + 2.0 * zz
            twice_xy, twice_xz, twice_yx = 2.0 * xy, 2.0 * xz, 2.0 * yx
            twice_yz, twice_zx, twice_zy = 2.0 * yz, 2.0 * zx, 2.0 * zy
            pull = relax * spring

            def substep(_, parts):
                cxx, cxy, cxz, cyy, cyz, czz = parts
                room = extension - (cxx + cyy + czz)
                scale = room * (1.0 / (room + pull))
                nxx = twice_xx * cxx + twice_xy * cxy + twice_xz * cxz + relax
                nyy = twice_yx * cxy + twice_yy * cyy + twice_yz * cyz + relax
                nzz = twice_zx * cxz + twice_zy * cyz + twice_zz * czz + relax
                nxy = both_xy * cxy + xy * cyy + xz * cyz + yx * cxx + yz * cxz
                nxz = both_xz * cxz + xy * cyz + xz * czz + zx * cxx + zy * cxy
                nyz = both_yz * cyz + yx * cxz + yz * czz + zx * cxy + zy * cyy
                return tuple(n * scale for n in (nxx, nxy, nxz, nyy, nyz, nzz))

            def several(_, parts):
                for _ in range(UNROLL):
                    parts = substep(_, parts)
                return parts

            parts = tuple(conf_ref[(slot, i) + here] for i in range(6))
            parts = lax.fori_loop(0, substeps[slot] // UNROLL, several, parts)
            parts = lax.fori_loop(0, substeps[slot] % UNROLL, substep, parts)
            for i in range(6):
                new_ref[(slot, i) + here] = parts[i]
            weight = rate / modes_total
            factor = weight * spring / (extension - (parts[0] + parts[3] + parts[5]))
            terms = [factor * part - (weight if i in (0, 3, 5) else 0.0) for i, part in enumerate(parts)]
            total = terms if total is None else [a + b for a, b in zip(total, terms)]
        for i in range(6):
            value = total[i] if added_ref is None else total[i] + added_ref[(i,) + here]
            stress_ref[(i,) + here] = value
        return carry

    lax.fori_loop(0, rows // 8 * across, tile, 0)


def columns_of(target, columns):
    return pl.ds(pl.multiple_of(target * columns, columns), columns)


def fetch(target, conf_hbm, grad_hbm, conf_ref, grad_ref, sems):
    span = columns_of(target, conf_ref.shape[3])
    return [
        pltpu.make_async_copy(conf_hbm.at[:, :, :, span], conf_ref, sems.at[0]),
        pltpu.make_async_copy(grad_hbm.at[:, :, span], grad_ref, sems.at[1]),
    ]


def start(copies):
    for copy in copies:
        copy.start()


def wait(copies):
    for copy in copies:
        copy.wait()


def first_kernel(now, later, modes, runs, mode_ref, counts_hbm, ids_hbm, conf_hbm, grad_hbm, *refs):
    n, m = len(now), len(later)
    (stress_ref,), news, confs, grads, (facts_ref,), held, slopes, (counts_ref, ids_ref, sems) = split(refs, [1, n, m, m, 1, n, n, 3])
    place = mode_ref[0]
    mode = place // 2
    slots = news[0].shape[0]
    small = [
        pltpu.make_async_copy(counts_hbm, counts_ref, sems.at[0]),
        pltpu.make_async_copy(ids_hbm, ids_ref, sems.at[1]),
    ]
    fetches = [
        fetch(partner(place, step, modes, runs), conf_hbm, grad_hbm, conf, grad, sems.at[2 * k + 2 : 2 * k + 4])
        for k, (step, conf, grad) in enumerate(zip(now + later, held + confs, slopes + grads))
    ]
    start(small)
    for copies in fetches:
        start(copies)
    wait(small)
    for slot in range(slots):
        order = ids_ref[mode * slots + slot] + 1
        facts_ref[slot] = jnp.full((8, 128), counts_ref[mode * slots + slot], jnp.int32)
        facts_ref[slots + slot] = jnp.full((8, 128), order * order, jnp.int32)
    for k in range(n):
        wait(fetches[k])
        advance_block(float(counts_hbm.shape[0]), facts_ref, held[k], slopes[k], news[k], stress_ref.at[k])
    for copies in fetches[n:]:
        wait(copies)


def middle_kernel(step, joined, later, ties, modes, runs, modes_total, mode_ref, facts_ref, conf_hbm, grad_hbm, *refs):
    (held, slope), added, _, (stress_ref, new_ref, conf_ref, grad_ref, sems) = split(refs, [2, joined, ties, 5])
    copies = fetch(partner(mode_ref[0], later, modes, runs), conf_hbm, grad_hbm, conf_ref, grad_ref, sems)
    start(copies)
    advance_block(modes_total, facts_ref, held, slope, new_ref, stress_ref, added[0].at[1 - step[0]] if added else None)
    wait(copies)


def last_kernel(steps, modes, runs, modes_total, mode_ref, facts_ref, *refs):
    (held, slope), done, (stress_ref, out_hbm, new_ref, sems) = split(refs, [2, len(steps) - 1, 4])
    copies = []
    for k, (step, ref) in enumerate(zip(steps, done + [new_ref])):
        span = columns_of(partner(mode_ref[0], step, modes, runs), ref.shape[3])
        copies.append(pltpu.make_async_copy(ref, out_hbm.at[:, :, :, span], sems.at[k]))
    start(copies[:-1])
    advance_block(modes_total, facts_ref, held, slope, new_ref, stress_ref)
    copies[-1].start()
    wait(copies)


def split(refs, sizes):
    found, at = [], 0
    for size in sizes:
        found.append(list(refs[at : at + size]))
        at += size
    return found


def advance(mode, counts, ids, conformation, gradient, modes, runs, send):
    slots, comps, rows, columns = conformation.shape
    block = columns // modes
    calls = plan(modes // runs)
    total = float(counts.shape[0])
    smem, vmem, hbm = (pl.BlockSpec(memory_space=s) for s in (pltpu.SMEM, pltpu.VMEM, pltpu.HBM))
    stress = jax.ShapeDtypeStruct((comps, rows, block), F32)
    new = pltpu.VMEM((slots, comps, rows, block), F32)
    grad = pltpu.VMEM((8, rows, block), F32)
    dma = pltpu.SemaphoreType.DMA
    cost = pl.CostEstimate(flops=1024, bytes_accessed=1024, transcendentals=0)
    counts, ids, conformation, gradient = (
        pltpu.with_memory_space_constraint(x, pltpu.HBM) for x in (counts, ids, conformation, gradient)
    )
    now, later = calls[0], calls[1]
    n = len(now)
    out = pl.pallas_call(
        lambda *refs: first_kernel(now, later, modes, runs, *refs),
        in_specs=[smem] + [hbm] * 4,
        out_specs=[vmem] * (n + 4),
        out_shape=[jax.ShapeDtypeStruct((n,) + stress.shape, F32)]
        + [new] * (n + 1)
        + [grad, pltpu.VMEM((2 * slots, 8, 128), jnp.int32)],
        scratch_shapes=[new] * n + [grad] * n + [pltpu.SMEM(counts.shape, jnp.int32), pltpu.SMEM(ids.shape, jnp.int32)]
        + [dma((2 * n + 4,))],
        compiler_params=pltpu.CompilerParams(vmem_limit_bytes=FIRST_LIMIT),
        cost_estimate=cost,
        name="advance_first",
    )(mode, counts, ids, conformation, gradient)
    value, news, held, facts = out[0], list(out[1 : n + 1]), out[n + 1 : n + 3], out[n + 3]
    far, parts = send((0, 1), value), []
    for k in range(1, len(calls) - 1):
        step, later = calls[k][0], calls[k + 1][0]
        added = [far] if step[1] == 1 else []
        order = [news[-1]]
        out = pl.pallas_call(
            lambda *refs, step=step, later=later, joined=len(added): middle_kernel(step, joined, later, 1, modes, runs, total, *refs),
            in_specs=[smem, vmem, hbm, hbm] + [vmem] * (3 + len(added)),
            out_specs=[vmem] * 4,
            out_shape=[stress, new, new, grad],
            scratch_shapes=[dma((2,))],
            compiler_params=pltpu.CompilerParams(vmem_limit_bytes=LIMIT),
            cost_estimate=cost,
            name="advance_middle",
        )(mode, facts, conformation, gradient, *held, *added, *order)
        parts.append(send(step, out[0]))
        news.append(out[1])
        held = out[2:]
    steps = [step for call in calls for step in call]
    value, stored = pl.pallas_call(
        lambda *refs: last_kernel(steps, modes, runs, total, *refs),
        in_specs=[smem, vmem] + [vmem] * (2 + len(news)),
        out_specs=[vmem, hbm],
        out_shape=[stress, jax.ShapeDtypeStruct(conformation.shape, F32)],
        scratch_shapes=[new, dma((modes,))],
        compiler_params=pltpu.CompilerParams(vmem_limit_bytes=LIMIT),
        cost_estimate=cost,
        name="advance_last",
    )(mode, facts, *held, *news)
    return parts + [value], stored


def pack_kernel(share, *refs):
    parts_refs, out_ref = refs[:-1], refs[-1]
    comps, rows, block = parts_refs[0].shape
    group = 128 // share
    lane = lax.broadcasted_iota(jnp.int32, (8, 128), 1) // share
    for row in range(0, rows, 8):
        for tile in range(0, block, 128):
            sums = []
            for comp in range(comps):
                sums.append(sum(ref[comp, row : row + 8, tile : tile + 128] for ref in parts_refs))
            sums += [jnp.zeros((8, 128), F32)] * (group - comps)
            distance = 1
            while distance < group:
                low = lane & distance == 0
                for i in range(group):
                    if i & distance == 0:
                        first, second = sums[i], sums[i + distance]
                        sums[i] = jnp.where(low, first, pltpu.roll(second, distance * share, 1))
                        sums[i + distance] = jnp.where(low, pltpu.roll(first, 128 - distance * share, 1), second)
                distance *= 2
            for member in range(group):
                out_ref[tile // share + member, row : row + 8, :] = sums[member]


def pack(parts, pencils):
    comps, rows, block = parts[0].shape
    share = block // pencils
    return pl.pallas_call(
        lambda *refs: pack_kernel(share, *refs),
        out_shape=jax.ShapeDtypeStruct((pencils, rows, 128), F32),
        compiler_params=pltpu.CompilerParams(vmem_limit_bytes=12 * 2**20),
        cost_estimate=pl.CostEstimate(flops=400 * 1024, bytes_accessed=2**21, transcendentals=0),
        name="pack",
    )(*parts)


def transform_kernel(comps, share, values_ref, high_ref, low_ref, out_ref):
    values = values_ref[...]
    high = values.astype(jnp.bfloat16)
    low = (values - high.astype(F32)).astype(jnp.bfloat16)

    both = jnp.dot(high_ref[...], jnp.concatenate([high, low], axis=1), preferred_element_type=F32)
    cross = jnp.dot(low_ref[...], high, preferred_element_type=F32)
    width = values.shape[1]
    result = both[:, :width] + (both[:, width:] + cross)
    result = result.T
    for comp in range(comps):
        out_ref[comp] = result[comp * share : (comp + 1) * share]


def transform(values, comps, share):
    points = values.shape[0]
    high, low = split_table(points)
    return pl.pallas_call(
        lambda *refs: transform_kernel(comps, share, *refs),
        out_shape=jax.ShapeDtypeStruct((comps, share, points), F32),
        compiler_params=pltpu.CompilerParams(vmem_limit_bytes=12 * 2**20),
        cost_estimate=pl.CostEstimate(flops=2 * 3 * 128 * 512 * 512, bytes_accessed=2**21, transcendentals=0),
        name="transform",
    )(values, high, low)


def per_device(runs, conformation, gradient, counts, mode_ids):
    slots, comps, rows, columns = conformation.shape
    modes, pencils = lax.axis_size("mode"), lax.axis_size("pencil")
    place = lax.axis_index("mode") * 2 + lax.axis_index("pencil") % 2
    place = place.astype(jnp.int32).reshape(1)

    def send(step, value):
        pairs = [
            (m * pencils + p, partner(m * 2 + p % 2, step, modes, runs) * pencils + p)
            for m in range(modes)
            for p in range(pencils)
        ]
        return lax.ppermute(value, ("mode", "pencil"), pairs)

    parts, new_conformation = advance(place, counts, mode_ids, conformation, gradient, modes, runs, send)
    packed = pack(parts, pencils)
    planes = lax.all_to_all(packed, "pencil", split_axis=0, concat_axis=0, tiled=True)
    share = columns // modes // pencils
    return new_conformation, transform(planes.reshape(rows * pencils, 128), comps, share)


def solution(mesh):
    in_specs = (P("mode", None, "pencil", None), P(None, "pencil", None), P(), P())
    out_specs = (P("mode", None, "pencil", None), P(None, ("mode", "pencil"), None))
    return jax.shard_map(
        functools.partial(per_device, 2), mesh=mesh, in_specs=in_specs, out_specs=out_specs, check_vma=False
    )
```

```python
import functools
import math

import jax
import jax.numpy as jnp
import ml_dtypes
import numpy as np
from jax import lax
from jax.experimental import pallas as pl
from jax.experimental.pallas import tpu as pltpu
from jax.sharding import PartitionSpec as P

step_time = 0.25
extension = 900.0
spring = extension - 3.0
F32 = jnp.float32
WIDTH = 512
UNROLL = 2
LIMIT = 16 * 2**20
FIRST_LIMIT = 52 * 2**20


def transform_table(points_count):
    final_index = points_count - 1
    position = np.arange(points_count)
    product = position[:, None] * position[None, :] % (2 * final_index)
    edge = np.where((position == 0) | (position == final_index), math.sqrt(0.5), 1.0)
    return math.sqrt(2.0 / final_index) * edge[:, None] * edge[None, :] * np.cos(np.pi * product / final_index)


def split_table(points_count):
    table = transform_table(points_count)
    high = table.astype(ml_dtypes.bfloat16)
    low = (table - high.astype(np.float64)).astype(ml_dtypes.bfloat16)
    return high, low


def plan(rings):
    assert rings == 4
    return [[(1, 2), (0, 2)], [(1, 0)], [(0, 3)], [(1, 3)], [(1, 1)], [(0, 1)], [(0, 0)]]


def partner(place, offset, modes, runs):
    mode, core = place // 2, place % 2
    rings = modes // runs
    ring = (mode // runs + rings + (1 - 2 * core) * offset[1]) % rings
    return ring * runs + (mode % runs + offset[0]) % runs


def wide(value, width):
    return jnp.concatenate([value] * (width // value.shape[1]), axis=1)


def advance_block(modes_total, facts_ref, conf_ref, grad_ref, new_ref, stress_ref, added_ref=None):
    slots, _, rows, columns = new_ref.shape
    width = min(WIDTH, columns)
    across = columns // width

    substeps = [jnp.max(facts_ref[slot]) for slot in range(slots)]

    def tile(index, carry):
        row = pl.multiple_of(index // across * 8, 8)
        column = pl.multiple_of(index % across * width, width)
        here = (pl.ds(row, 8), pl.ds(column, width))
        total = None
        for slot in range(slots):
            rate = wide(facts_ref[slots + slot].astype(F32), width)
            step = step_time / wide(facts_ref[slot].astype(F32), width)
            relax = step * rate
            xx, xy, xz, yx, yy, yz, zx, zy = (grad_ref[(i,) + here] * step for i in range(8))
            zz = -(xx + yy)
            both_xy, both_xz, both_yz = 1.0 - zz, 1.0 - yy, 1.0 - xx
            twice_xx, twice_yy, twice_zz = 1.0 + 2.0 * xx, 1.0 + 2.0 * yy, 1.0 + 2.0 * zz
            twice_xy, twice_xz, twice_yx = 2.0 * xy, 2.0 * xz, 2.0 * yx
            twice_yz, twice_zx, twice_zy = 2.0 * yz, 2.0 * zx, 2.0 * zy
            pull = relax * spring

            def substep(_, parts):
                cxx, cxy, cxz, cyy, cyz, czz = parts
                room = extension - (cxx + cyy + czz)
                scale = room * (1.0 / (room + pull))
                nxx = twice_xx * cxx + twice_xy * cxy + twice_xz * cxz + relax
                nyy = twice_yx * cxy + twice_yy * cyy + twice_yz * cyz + relax
                nzz = twice_zx * cxz + twice_zy * cyz + twice_zz * czz + relax
                nxy = both_xy * cxy + xy * cyy + xz * cyz + yx * cxx + yz * cxz
                nxz = both_xz * cxz + xy * cyz + xz * czz + zx * cxx + zy * cxy
                nyz = both_yz * cyz + yx * cxz + yz * czz + zx * cxy + zy * cyy
                return tuple(n * scale for n in (nxx, nxy, nxz, nyy, nyz, nzz))

            def several(_, parts):
                for _ in range(UNROLL):
                    parts = substep(_, parts)
                return parts

            parts = tuple(conf_ref[(slot, i) + here] for i in range(6))
            parts = lax.fori_loop(0, substeps[slot] // UNROLL, several, parts)
            parts = lax.fori_loop(0, substeps[slot] % UNROLL, substep, parts)
            for i in range(6):
                new_ref[(slot, i) + here] = parts[i]
            weight = rate / modes_total
            factor = weight * spring / (extension - (parts[0] + parts[3] + parts[5]))
            terms = [factor * part - (weight if i in (0, 3, 5) else 0.0) for i, part in enumerate(parts)]
            total = terms if total is None else [a + b for a, b in zip(total, terms)]
        for i in range(6):
            value = total[i] if added_ref is None else total[i] + added_ref[(i,) + here]
            stress_ref[(i,) + here] = value
        return carry

    lax.fori_loop(0, rows // 8 * across, tile, 0)


def columns_of(target, columns):
    return pl.ds(pl.multiple_of(target * columns, columns), columns)


def fetch(target, conf_hbm, grad_hbm, conf_ref, grad_ref, sems):
    span = columns_of(target, conf_ref.shape[3])
    return [
        pltpu.make_async_copy(conf_hbm.at[:, :, :, span], conf_ref, sems.at[0]),
        pltpu.make_async_copy(grad_hbm.at[:, :, span], grad_ref, sems.at[1]),
    ]


def start(copies):
    for copy in copies:
        copy.start()


def wait(copies):
    for copy in copies:
        copy.wait()


def first_kernel(now, later, modes, runs, mode_ref, counts_hbm, ids_hbm, conf_hbm, grad_hbm, *refs):
    n, m = len(now), len(later)
    (stress_ref,), news, confs, grads, (facts_ref,), held, slopes, (counts_ref, ids_ref, sems) = split(refs, [1, n, m, m, 1, n, n, 3])
    place = mode_ref[0]
    mode = place // 2
    slots = news[0].shape[0]
    small = [
        pltpu.make_async_copy(counts_hbm, counts_ref, sems.at[0]),
        pltpu.make_async_copy(ids_hbm, ids_ref, sems.at[1]),
    ]
    fetches = [
        fetch(partner(place, step, modes, runs), conf_hbm, grad_hbm, conf, grad, sems.at[2 * k + 2 : 2 * k + 4])
        for k, (step, conf, grad) in enumerate(zip(now + later, held + confs, slopes + grads))
    ]
    start(small)
    for copies in fetches:
        start(copies)
    wait(small)
    for slot in range(slots):
        order = ids_ref[mode * slots + slot] + 1
        facts_ref[slot] = jnp.full((8, 128), counts_ref[mode * slots + slot], jnp.int32)
        facts_ref[slots + slot] = jnp.full((8, 128), order * order, jnp.int32)
    for k in range(n):
        wait(fetches[k])
        advance_block(float(counts_hbm.shape[0]), facts_ref, held[k], slopes[k], news[k], stress_ref.at[k])
    for copies in fetches[n:]:
        wait(copies)


def middle_kernel(step, joined, later, ties, modes, runs, modes_total, mode_ref, facts_ref, conf_hbm, grad_hbm, *refs):
    (held, slope), added, _, (stress_ref, new_ref, conf_ref, grad_ref, sems) = split(refs, [2, joined, ties, 5])
    copies = fetch(partner(mode_ref[0], later, modes, runs), conf_hbm, grad_hbm, conf_ref, grad_ref, sems)
    start(copies)
    advance_block(modes_total, facts_ref, held, slope, new_ref, stress_ref, added[0].at[1 - step[0]] if added else None)
    wait(copies)


def last_kernel(steps, modes, runs, modes_total, mode_ref, facts_ref, *refs):
    (held, slope), done, (stress_ref, out_hbm, new_ref, sems) = split(refs, [2, len(steps) - 1, 4])
    copies = []
    for k, (step, ref) in enumerate(zip(steps, done + [new_ref])):
        span = columns_of(partner(mode_ref[0], step, modes, runs), ref.shape[3])
        copies.append(pltpu.make_async_copy(ref, out_hbm.at[:, :, :, span], sems.at[k]))
    start(copies[:-1])
    advance_block(modes_total, facts_ref, held, slope, new_ref, stress_ref)
    copies[-1].start()
    wait(copies)


def split(refs, sizes):
    found, at = [], 0
    for size in sizes:
        found.append(list(refs[at : at + size]))
        at += size
    return found


def advance(mode, counts, ids, conformation, gradient, modes, runs, send):
    slots, comps, rows, columns = conformation.shape
    block = columns // modes
    calls = plan(modes // runs)
    total = float(counts.shape[0])
    smem, vmem, hbm = (pl.BlockSpec(memory_space=s) for s in (pltpu.SMEM, pltpu.VMEM, pltpu.HBM))
    stress = jax.ShapeDtypeStruct((comps, rows, block), F32)
    new = pltpu.VMEM((slots, comps, rows, block), F32)
    grad = pltpu.VMEM((8, rows, block), F32)
    dma = pltpu.SemaphoreType.DMA
    cost = pl.CostEstimate(flops=1024, bytes_accessed=1024, transcendentals=0)
    counts, ids, conformation, gradient = (
        pltpu.with_memory_space_constraint(x, pltpu.HBM) for x in (counts, ids, conformation, gradient)
    )
    now, later = calls[0], calls[1]
    n = len(now)
    out = pl.pallas_call(
        lambda *refs: first_kernel(now, later, modes, runs, *refs),
        in_specs=[smem] + [hbm] * 4,
        out_specs=[vmem] * (n + 4),
        out_shape=[jax.ShapeDtypeStruct((n,) + stress.shape, F32)]
        + [new] * (n + 1)
        + [grad, pltpu.VMEM((2 * slots, 8, 128), jnp.int32)],
        scratch_shapes=[new] * n + [grad] * n + [pltpu.SMEM(counts.shape, jnp.int32), pltpu.SMEM(ids.shape, jnp.int32)]
        + [dma((2 * n + 4,))],
        compiler_params=pltpu.CompilerParams(vmem_limit_bytes=FIRST_LIMIT),
        cost_estimate=cost,
        name="advance_first",
    )(mode, counts, ids, conformation, gradient)
    value, news, held, facts = out[0], list(out[1 : n + 1]), out[n + 1 : n + 3], out[n + 3]
    far, parts = send((0, 1), value), []
    for k in range(1, len(calls) - 1):
        step, later = calls[k][0], calls[k + 1][0]
        added = [far] if step[1] == 1 else []
        order = [news[-1]]
        out = pl.pallas_call(
            lambda *refs, step=step, later=later, joined=len(added): middle_kernel(step, joined, later, 1, modes, runs, total, *refs),
            in_specs=[smem, vmem, hbm, hbm] + [vmem] * (3 + len(added)),
            out_specs=[vmem] * 4,
            out_shape=[stress, new, new, grad],
            scratch_shapes=[dma((2,))],
            compiler_params=pltpu.CompilerParams(vmem_limit_bytes=LIMIT),
            cost_estimate=cost,
            name="advance_middle",
        )(mode, facts, conformation, gradient, *held, *added, *order)
        parts.append(send(step, out[0]))
        news.append(out[1])
        held = out[2:]
    steps = [step for call in calls for step in call]
    value, stored = pl.pallas_call(
        lambda *refs: last_kernel(steps, modes, runs, total, *refs),
        in_specs=[smem, vmem] + [vmem] * (2 + len(news)),
        out_specs=[vmem, hbm],
        out_shape=[stress, jax.ShapeDtypeStruct(conformation.shape, F32)],
        scratch_shapes=[new, dma((modes,))],
        compiler_params=pltpu.CompilerParams(vmem_limit_bytes=LIMIT),
        cost_estimate=cost,
        name="advance_last",
    )(mode, facts, *held, *news)
    return parts + [value], stored


def pack_kernel(share, *refs):
    parts_refs, out_ref = refs[:-1], refs[-1]
    comps, rows, block = parts_refs[0].shape
    group = 128 // share
    lane = lax.broadcasted_iota(jnp.int32, (8, 128), 1) // share
    for row in range(0, rows, 8):
        for tile in range(0, block, 128):
            sums = []
            for comp in range(comps):
                sums.append(sum(ref[comp, row : row + 8, tile : tile + 128] for ref in parts_refs))
            sums += [jnp.zeros((8, 128), F32)] * (group - comps)
            distance = 1
            while distance < group:
                low = lane & distance == 0
                for i in range(group):
                    if i & distance == 0:
                        first, second = sums[i], sums[i + distance]
                        sums[i] = jnp.where(low, first, pltpu.roll(second, distance * share, 1))
                        sums[i + distance] = jnp.where(low, pltpu.roll(first, 128 - distance * share, 1), second)
                distance *= 2
            for member in range(group):
                out_ref[tile // share + member, row : row + 8, :] = sums[member]


def pack(parts, pencils):
    comps, rows, block = parts[0].shape
    share = block // pencils
    return pl.pallas_call(
        lambda *refs: pack_kernel(share, *refs),
        out_shape=jax.ShapeDtypeStruct((pencils, rows, 128), F32),
        compiler_params=pltpu.CompilerParams(vmem_limit_bytes=12 * 2**20),
        cost_estimate=pl.CostEstimate(flops=400 * 1024, bytes_accessed=2**21, transcendentals=0),
        name="pack",
    )(*parts)


def transform_kernel(comps, share, values_ref, high_ref, low_ref, out_ref):
    values = values_ref[...]
    high = values.astype(jnp.bfloat16)
    low = (values - high.astype(F32)).astype(jnp.bfloat16)

    both = jnp.dot(high_ref[...], jnp.concatenate([high, low], axis=1), preferred_element_type=F32)
    cross = jnp.dot(low_ref[...], high, preferred_element_type=F32)
    width = values.shape[1]
    result = both[:, :width] + (both[:, width:] + cross)
    result = result.T
    for comp in range(comps):
        out_ref[comp] = result[comp * share : (comp + 1) * share]


def transform(values, comps, share):
    points = values.shape[0]
    high, low = split_table(points)
    return pl.pallas_call(
        lambda *refs: transform_kernel(comps, share, *refs),
        out_shape=jax.ShapeDtypeStruct((comps, share, points), F32),
        compiler_params=pltpu.CompilerParams(vmem_limit_bytes=12 * 2**20),
        cost_estimate=pl.CostEstimate(flops=2 * 3 * 128 * 512 * 512, bytes_accessed=2**21, transcendentals=0),
        name="transform",
    )(values, high, low)


def per_device(runs, conformation, gradient, counts, mode_ids):
    slots, comps, rows, columns = conformation.shape
    modes, pencils = lax.axis_size("mode"), lax.axis_size("pencil")
    place = lax.axis_index("mode") * 2 + lax.axis_index("pencil") % 2
    place = place.astype(jnp.int32).reshape(1)

    def send(step, value):
        pairs = [
            (m * pencils + p, partner(m * 2 + p % 2, step, modes, runs) * pencils + p)
            for m in range(modes)
            for p in range(pencils)
        ]
        return lax.ppermute(value, ("mode", "pencil"), pairs)

    parts, new_conformation = advance(place, counts, mode_ids, conformation, gradient, modes, runs, send)
    packed = pack(parts, pencils)
    planes = lax.all_to_all(packed, "pencil", split_axis=0, concat_axis=0, tiled=True)
    share = columns // modes // pencils
    return new_conformation, transform(planes.reshape(rows * pencils, 128), comps, share)


def solution(mesh):
    in_specs = (P("mode", None, "pencil", None), P(None, "pencil", None), P(), P())
    out_specs = (P("mode", None, "pencil", None), P(None, ("mode", "pencil"), None))
    return jax.shard_map(
        functools.partial(per_device, 2), mesh=mesh, in_specs=in_specs, out_specs=out_specs, check_vma=False
    )
```

```python
import functools
import math

import jax
import jax.numpy as jnp
import ml_dtypes
import numpy as np
from jax import lax
from jax.experimental import pallas as pl
from jax.experimental.pallas import tpu as pltpu
from jax.sharding import PartitionSpec as P

step_time = 0.25
extension = 900.0
spring = extension - 3.0
F32 = jnp.float32
WIDTH = 512
UNROLL = 2
LIMIT = 16 * 2**20
FIRST_LIMIT = 52 * 2**20


def transform_table(points_count):
    final_index = points_count - 1
    position = np.arange(points_count)
    product = position[:, None] * position[None, :] % (2 * final_index)
    edge = np.where((position == 0) | (position == final_index), math.sqrt(0.5), 1.0)
    return math.sqrt(2.0 / final_index) * edge[:, None] * edge[None, :] * np.cos(np.pi * product / final_index)


def split_table(points_count):
    table = transform_table(points_count)
    high = table.astype(ml_dtypes.bfloat16)
    low = (table - high.astype(np.float64)).astype(ml_dtypes.bfloat16)
    return high, low


def plan(rings):
    assert rings == 4
    return [[(1, 2), (0, 2)], [(1, 0)], [(0, 3)], [(1, 3)], [(1, 1)], [(0, 1)], [(0, 0)]]


def partner(place, offset, modes, runs):
    mode, core = place // 2, place % 2
    rings = modes // runs
    ring = (mode // runs + rings + (1 - 2 * core) * offset[1]) % rings
    return ring * runs + (mode % runs + offset[0]) % runs


def wide(value, width):
    return jnp.concatenate([value] * (width // value.shape[1]), axis=1)


def advance_block(modes_total, facts_ref, conf_ref, grad_ref, new_ref, stress_ref, added_ref=None):
    slots, _, rows, columns = new_ref.shape
    width = min(WIDTH, columns)
    across = columns // width

    substeps = [jnp.max(facts_ref[slot]) for slot in range(slots)]

    def tile(index, carry):
        row = pl.multiple_of(index // across * 8, 8)
        column = pl.multiple_of(index % across * width, width)
        here = (pl.ds(row, 8), pl.ds(column, width))
        total = None
        for slot in range(slots):
            rate = wide(facts_ref[slots + slot].astype(F32), width)
            step = step_time / wide(facts_ref[slot].astype(F32), width)
            relax = step * rate
            xx, xy, xz, yx, yy, yz, zx, zy = (grad_ref[(i,) + here] * step for i in range(8))
            zz = -(xx + yy)
            both_xy, both_xz, both_yz = 1.0 - zz, 1.0 - yy, 1.0 - xx
            twice_xx, twice_yy, twice_zz = 1.0 + 2.0 * xx, 1.0 + 2.0 * yy, 1.0 + 2.0 * zz
            twice_xy, twice_xz, twice_yx = 2.0 * xy, 2.0 * xz, 2.0 * yx
            twice_yz, twice_zx, twice_zy = 2.0 * yz, 2.0 * zx, 2.0 * zy
            pull = relax * spring

            def substep(_, parts):
                cxx, cxy, cxz, cyy, cyz, czz = parts
                room = extension - (cxx + cyy + czz)
                scale = room * (1.0 / (room + pull))
                nxx = twice_xx * cxx + twice_xy * cxy + twice_xz * cxz + relax
                nyy = twice_yx * cxy + twice_yy * cyy + twice_yz * cyz + relax
                nzz = twice_zx * cxz + twice_zy * cyz + twice_zz * czz + relax
                nxy = both_xy * cxy + xy * cyy + xz * cyz + yx * cxx + yz * cxz
                nxz = both_xz * cxz + xy * cyz + xz * czz + zx * cxx + zy * cxy
                nyz = both_yz * cyz + yx * cxz + yz * czz + zx * cxy + zy * cyy
                return tuple(n * scale for n in (nxx, nxy, nxz, nyy, nyz, nzz))

            def several(_, parts):
                for _ in range(UNROLL):
                    parts = substep(_, parts)
                return parts

            parts = tuple(conf_ref[(slot, i) + here] for i in range(6))
            parts = lax.fori_loop(0, substeps[slot] // UNROLL, several, parts)
            parts = lax.fori_loop(0, substeps[slot] % UNROLL, substep, parts)
            for i in range(6):
                new_ref[(slot, i) + here] = parts[i]
            weight = rate / modes_total
            factor = weight * spring / (extension - (parts[0] + parts[3] + parts[5]))
            terms = [factor * part - (weight if i in (0, 3, 5) else 0.0) for i, part in enumerate(parts)]
            total = terms if total is None else [a + b for a, b in zip(total, terms)]
        for i in range(6):
            value = total[i] if added_ref is None else total[i] + added_ref[(i,) + here]
            stress_ref[(i,) + here] = value
        return carry

    lax.fori_loop(0, rows // 8 * across, tile, 0)


def columns_of(target, columns):
    return pl.ds(pl.multiple_of(target * columns, columns), columns)


def fetch(target, conf_hbm, grad_hbm, conf_ref, grad_ref, sems):
    span = columns_of(target, conf_ref.shape[3])
    return [
        pltpu.make_async_copy(conf_hbm.at[:, :, :, span], conf_ref, sems.at[0]),
        pltpu.make_async_copy(grad_hbm.at[:, :, span], grad_ref, sems.at[1]),
    ]


def start(copies):
    for copy in copies:
        copy.start()


def wait(copies):
    for copy in copies:
        copy.wait()


def first_kernel(now, later, modes, runs, mode_ref, counts_hbm, ids_hbm, conf_hbm, grad_hbm, *refs):
    n, m = len(now), len(later)
    (stress_ref,), news, confs, grads, (facts_ref,), held, slopes, (counts_ref, ids_ref, sems) = split(refs, [1, n, m, m, 1, n, n, 3])
    place = mode_ref[0]
    mode = place // 2
    slots = news[0].shape[0]
    small = [
        pltpu.make_async_copy(counts_hbm, counts_ref, sems.at[0]),
        pltpu.make_async_copy(ids_hbm, ids_ref, sems.at[1]),
    ]
    fetches = [
        fetch(partner(place, step, modes, runs), conf_hbm, grad_hbm, conf, grad, sems.at[2 * k + 2 : 2 * k + 4])
        for k, (step, conf, grad) in enumerate(zip(now + later, held + confs, slopes + grads))
    ]
    start(small + fetches[0])
    wait(small)
    for slot in range(slots):
        order = ids_ref[mode * slots + slot] + 1
        facts_ref[slot] = jnp.full((8, 128), counts_ref[mode * slots + slot], jnp.int32)
        facts_ref[slots + slot] = jnp.full((8, 128), order * order, jnp.int32)
    wait(fetches[0])
    for copies in fetches[1:]:
        start(copies)
    for k in range(n):
        if k > 0:
            wait(fetches[k])
        advance_block(float(counts_hbm.shape[0]), facts_ref, held[k], slopes[k], news[k], stress_ref.at[k])
    for copies in fetches[n:]:
        wait(copies)


def middle_kernel(step, joined, later, ties, modes, runs, modes_total, mode_ref, facts_ref, conf_hbm, grad_hbm, *refs):
    (held, slope), added, _, (stress_ref, new_ref, conf_ref, grad_ref, sems) = split(refs, [2, joined, ties, 5])
    copies = fetch(partner(mode_ref[0], later, modes, runs), conf_hbm, grad_hbm, conf_ref, grad_ref, sems)
    start(copies)
    advance_block(modes_total, facts_ref, held, slope, new_ref, stress_ref, added[0].at[1 - step[0]] if added else None)
    wait(copies)


def last_kernel(steps, modes, runs, modes_total, mode_ref, facts_ref, *refs):
    (held, slope), done, (stress_ref, out_hbm, new_ref, sems) = split(refs, [2, len(steps) - 1, 4])
    copies = []
    for k, (step, ref) in enumerate(zip(steps, done + [new_ref])):
        span = columns_of(partner(mode_ref[0], step, modes, runs), ref.shape[3])
        copies.append(pltpu.make_async_copy(ref, out_hbm.at[:, :, :, span], sems.at[k]))
    start(copies[:-1])
    advance_block(modes_total, facts_ref, held, slope, new_ref, stress_ref)
    copies[-1].start()
    wait(copies)


def split(refs, sizes):
    found, at = [], 0
    for size in sizes:
        found.append(list(refs[at : at + size]))
        at += size
    return found


def advance(mode, counts, ids, conformation, gradient, modes, runs, send):
    slots, comps, rows, columns = conformation.shape
    block = columns // modes
    calls = plan(modes // runs)
    total = float(counts.shape[0])
    smem, vmem, hbm = (pl.BlockSpec(memory_space=s) for s in (pltpu.SMEM, pltpu.VMEM, pltpu.HBM))
    stress = jax.ShapeDtypeStruct((comps, rows, block), F32)
    new = pltpu.VMEM((slots, comps, rows, block), F32)
    grad = pltpu.VMEM((8, rows, block), F32)
    dma = pltpu.SemaphoreType.DMA
    cost = pl.CostEstimate(flops=1024, bytes_accessed=1024, transcendentals=0)
    counts, ids, conformation, gradient = (
        pltpu.with_memory_space_constraint(x, pltpu.HBM) for x in (counts, ids, conformation, gradient)
    )
    now, later = calls[0], calls[1]
    n = len(now)
    out = pl.pallas_call(
        lambda *refs: first_kernel(now, later, modes, runs, *refs),
        in_specs=[smem] + [hbm] * 4,
        out_specs=[vmem] * (n + 4),
        out_shape=[jax.ShapeDtypeStruct((n,) + stress.shape, F32)]
        + [new] * (n + 1)
        + [grad, pltpu.VMEM((2 * slots, 8, 128), jnp.int32)],
        scratch_shapes=[new] * n + [grad] * n + [pltpu.SMEM(counts.shape, jnp.int32), pltpu.SMEM(ids.shape, jnp.int32)]
        + [dma((2 * n + 4,))],
        compiler_params=pltpu.CompilerParams(vmem_limit_bytes=FIRST_LIMIT),
        cost_estimate=cost,
        name="advance_first",
    )(mode, counts, ids, conformation, gradient)
    value, news, held, facts = out[0], list(out[1 : n + 1]), out[n + 1 : n + 3], out[n + 3]
    far, parts = send((0, 1), value), []
    for k in range(1, len(calls) - 1):
        step, later = calls[k][0], calls[k + 1][0]
        added = [far] if step[1] == 1 else []
        order = [news[-1]]
        out = pl.pallas_call(
            lambda *refs, step=step, later=later, joined=len(added): middle_kernel(step, joined, later, 1, modes, runs, total, *refs),
            in_specs=[smem, vmem, hbm, hbm] + [vmem] * (3 + len(added)),
            out_specs=[vmem] * 4,
            out_shape=[stress, new, new, grad],
            scratch_shapes=[dma((2,))],
            compiler_params=pltpu.CompilerParams(vmem_limit_bytes=LIMIT),
            cost_estimate=cost,
            name="advance_middle",
        )(mode, facts, conformation, gradient, *held, *added, *order)
        parts.append(send(step, out[0]))
        news.append(out[1])
        held = out[2:]
    steps = [step for call in calls for step in call]
    value, stored = pl.pallas_call(
        lambda *refs: last_kernel(steps, modes, runs, total, *refs),
        in_specs=[smem, vmem] + [vmem] * (2 + len(news)),
        out_specs=[vmem, hbm],
        out_shape=[stress, jax.ShapeDtypeStruct(conformation.shape, F32)],
        scratch_shapes=[new, dma((modes,))],
        compiler_params=pltpu.CompilerParams(vmem_limit_bytes=LIMIT),
        cost_estimate=cost,
        name="advance_last",
    )(mode, facts, *held, *news)
    return parts + [value], stored


def pack_kernel(share, *refs):
    parts_refs, out_ref = refs[:-1], refs[-1]
    comps, rows, block = parts_refs[0].shape
    group = 128 // share
    lane = lax.broadcasted_iota(jnp.int32, (8, 128), 1) // share
    for row in range(0, rows, 8):
        for tile in range(0, block, 128):
            sums = []
            for comp in range(comps):
                sums.append(sum(ref[comp, row : row + 8, tile : tile + 128] for ref in parts_refs))
            sums += [jnp.zeros((8, 128), F32)] * (group - comps)
            distance = 1
            while distance < group:
                low = lane & distance == 0
                for i in range(group):
                    if i & distance == 0:
                        first, second = sums[i], sums[i + distance]
                        sums[i] = jnp.where(low, first, pltpu.roll(second, distance * share, 1))
                        sums[i + distance] = jnp.where(low, pltpu.roll(first, 128 - distance * share, 1), second)
                distance *= 2
            for member in range(group):
                out_ref[tile // share + member, row : row + 8, :] = sums[member]


def pack(parts, pencils):
    comps, rows, block = parts[0].shape
    share = block // pencils
    return pl.pallas_call(
        lambda *refs: pack_kernel(share, *refs),
        out_shape=jax.ShapeDtypeStruct((pencils, rows, 128), F32),
        compiler_params=pltpu.CompilerParams(vmem_limit_bytes=12 * 2**20),
        cost_estimate=pl.CostEstimate(flops=400 * 1024, bytes_accessed=2**21, transcendentals=0),
        name="pack",
    )(*parts)


def transform_kernel(comps, share, values_ref, high_ref, low_ref, out_ref):
    values = values_ref[...]
    high = values.astype(jnp.bfloat16)
    low = (values - high.astype(F32)).astype(jnp.bfloat16)

    both = jnp.dot(high_ref[...], jnp.concatenate([high, low], axis=1), preferred_element_type=F32)
    cross = jnp.dot(low_ref[...], high, preferred_element_type=F32)
    width = values.shape[1]
    result = both[:, :width] + (both[:, width:] + cross)
    result = result.T
    for comp in range(comps):
        out_ref[comp] = result[comp * share : (comp + 1) * share]


def transform(values, comps, share):
    points = values.shape[0]
    high, low = split_table(points)
    return pl.pallas_call(
        lambda *refs: transform_kernel(comps, share, *refs),
        out_shape=jax.ShapeDtypeStruct((comps, share, points), F32),
        compiler_params=pltpu.CompilerParams(vmem_limit_bytes=12 * 2**20),
        cost_estimate=pl.CostEstimate(flops=2 * 3 * 128 * 512 * 512, bytes_accessed=2**21, transcendentals=0),
        name="transform",
    )(values, high, low)


def per_device(runs, conformation, gradient, counts, mode_ids):
    slots, comps, rows, columns = conformation.shape
    modes, pencils = lax.axis_size("mode"), lax.axis_size("pencil")
    place = lax.axis_index("mode") * 2 + lax.axis_index("pencil") % 2
    place = place.astype(jnp.int32).reshape(1)

    def send(step, value):
        pairs = [
            (m * pencils + p, partner(m * 2 + p % 2, step, modes, runs) * pencils + p)
            for m in range(modes)
            for p in range(pencils)
        ]
        return lax.ppermute(value, ("mode", "pencil"), pairs)

    parts, new_conformation = advance(place, counts, mode_ids, conformation, gradient, modes, runs, send)
    packed = pack(parts, pencils)
    planes = lax.all_to_all(packed, "pencil", split_axis=0, concat_axis=0, tiled=True)
    share = columns // modes // pencils
    return new_conformation, transform(planes.reshape(rows * pencils, 128), comps, share)


def solution(mesh):
    in_specs = (P("mode", None, "pencil", None), P(None, "pencil", None), P(), P())
    out_specs = (P("mode", None, "pencil", None), P(None, ("mode", "pencil"), None))
    return jax.shard_map(
        functools.partial(per_device, 2), mesh=mesh, in_specs=in_specs, out_specs=out_specs, check_vma=False
    )
```
